512 devices in a mesh: exp: 64 (over y, z), ten: 8 (over x, core).
Axes of the slice: x: 4, y: 8, z: 8, core: 2. Of those that a mesh axis runs over, the one named last changes fastest.
Arguments:
- tokens: bfloat16 [12288, 4096], P('exp', 'ten'), may hold values from -6 to 6
- output_grad: bfloat16 [12288, 4096], P('exp', 'ten'), may hold values from -3 to 3
- gate_weight: bfloat16 [64, 4096, 1024], P('exp', None, 'ten'), may hold values from -0.09375 to 0.09375
- up_weight: bfloat16 [64, 4096, 1024], P('exp', None, 'ten'), may hold values from -0.09375 to 0.09375
- down_weight: bfloat16 [64, 1024, 4096], P('exp', 'ten'), may hold values from -0.0625 to 0.0625
- chosen: int32 [8, 384], replicated, may hold values from 0 to 12287, as said below
- gate_values: float32 [8, 384], replicated, may hold values from 0.1 to 1
Outputs:
- grad_tokens: bfloat16 [12288, 4096], P('exp', 'ten')
- gate_grad: float32 [8, 384], replicated
The draws below stay inside these ranges and needn't reach their ends.
Inputs may be any that keep to these rules, and one draw needn't show every extreme that they name: `chosen`: each row names 384 different tokens. Of the block of 192 tokens held by one index of exp, a row names at most 8, and in every row exactly 8 for some index.
All inputs are finite; a program needn't handle non-finite values.
Results may differ from the reference program's by a relative error of at most 0.019.
Values may be sent and summed in bfloat16 or wider, within the bound.
No kernel may reach another device: no remote copies, remote signals or barrier semaphores. Data moves between devices by JAX's collectives and lax.ppermute only.
A program may use at most 64 MiB of HBM per device.

```python
import jax
import jax.numpy as jnp
from jax import lax

D = 4096
FF = 8192
SUB = 8
TOK_EXP = 192
EXPERTS = 8
TOKENS = 12288
CAP = 384
SHARE = 6
MOST = 8
N_TEN = 8


def draw_chosen(key, part):
    exp_count = TOKENS // TOK_EXP
    half = MOST - SHARE

    def one_expert(expert_key):
        key_order, key_spread, key_picks, key_shuffle = jax.random.split(expert_key, 4)
        order = jax.random.permutation(key_order, exp_count).astype(jnp.int32)
        spread = jax.random.randint(key_spread, (exp_count // 2,), 0, half + 1).astype(jnp.int32)
        spread = spread.at[0].set(half)
        by_place = jnp.stack([SHARE + spread, SHARE - spread], axis=1).reshape(-1).astype(jnp.int32)
        counts = jnp.zeros((exp_count,), jnp.int32).at[order].set(by_place)
        pick_keys = jax.random.split(key_picks, exp_count)
        picks = jax.vmap(lambda one_key: jax.random.permutation(one_key, TOK_EXP)[:MOST])(pick_keys).astype(jnp.int32)
        slot_ids = jnp.arange(MOST, dtype=jnp.int32)
        live = (slot_ids[None, :] < counts[:, None]).astype(jnp.int32)
        token_ids = picks + jnp.arange(exp_count, dtype=jnp.int32)[:, None] * TOK_EXP
        flat_live = live.reshape(-1)
        places = jnp.cumsum(flat_live) - 1
        places = jnp.where(flat_live == 1, places, CAP).astype(jnp.int32)
        listed = jnp.zeros((CAP + 1,), jnp.int32).at[places].set(token_ids.reshape(-1))[:CAP]
        shuffle = jax.random.permutation(key_shuffle, CAP)
        return listed[shuffle]
    expert_keys = jax.random.split(jax.random.fold_in(key, 7), EXPERTS)
    return jax.vmap(one_expert)(expert_keys)


def shard_levels(stream_key, shape, shards, low, top_value):
    loudness, own = 1.0, jax.random.fold_in(stream_key, 6)
    for axis_at, blocks in shards:
        heights = jnp.exp(jax.random.uniform(jax.random.fold_in(own, axis_at), (blocks,), jnp.float32, low / len(shards), top_value / len(shards)))
        loudness = loudness * jnp.repeat(heights, shape[axis_at] // blocks).reshape([-1 if axis == axis_at else 1 for axis in range(len(shape))])
    return loudness


def bell_draw(own_key, shape, deviation, limit, cuts=(), held_as=jnp.bfloat16):
    values = jax.random.normal(own_key, shape, jnp.float32) * deviation
    if len(cuts) > 0:
        values = shard_levels(own_key, shape, cuts, -0.22, 0.18) * values
    return jnp.clip(values, min=-limit, max=limit).astype(held_as)


def setup_inputs(seed: int = 0) -> dict:
    splits = jax.random.split(jax.random.key(seed), 8)
    return {
        "tokens": bell_draw(splits[0], (TOKENS, D), 1.0, 6.0, ((0, 64), (1, 8))),
        "output_grad": bell_draw(splits[1], (TOKENS, D), 0.5, 3.0, ((0, 64), (1, 8))),
        "gate_weight": bell_draw(splits[2], (EXPERTS * SUB, D, FF // SUB), D ** -0.5, 0.09375, ((0, 64), (2, 8))),
        "up_weight": bell_draw(splits[3], (EXPERTS * SUB, D, FF // SUB), D ** -0.5, 0.09375, ((0, 64), (2, 8))),
        "down_weight": bell_draw(splits[4], (EXPERTS * SUB, FF // SUB, D), FF ** -0.5, 0.0625, ((0, 64), (1, 8))),
        "chosen": draw_chosen(jax.random.fold_in(splits[7], 71), 0),
        "gate_values": jnp.clip(jax.random.uniform(splits[6], (EXPERTS, CAP), jnp.float32, 0.1, 1.0), 0.1, 1.0),
    }


def silu_parts(values):
    sig = jax.nn.sigmoid(values)
    return values * sig, sig * (1.0 + values * (1.0 - sig))


def reference(tokens, output_grad, gate_weight, up_weight, down_weight, chosen, gate_values):
    blocks = SUB * N_TEN
    ff_dev = FF // blocks
    contract = (((1,), (1,)), ((), ()))

    def per_expert(carry, expert):
        total, table = carry
        rows = chosen[expert]
        rows_in = tokens[rows]
        grads_in = output_grad[rows]
        gate_part = lax.dynamic_slice_in_dim(gate_weight, expert * SUB, SUB, 0)
        up_part = lax.dynamic_slice_in_dim(up_weight, expert * SUB, SUB, 0)
        down_part = lax.dynamic_slice_in_dim(down_weight, expert * SUB, SUB, 0)
        gate_full = jnp.transpose(gate_part, (1, 0, 2)).reshape(D, FF)
        up_full = jnp.transpose(up_part, (1, 0, 2)).reshape(D, FF)
        down_full = down_part.reshape(FF, D)
        pre_gate = jnp.dot(rows_in, gate_full, preferred_element_type=jnp.float32)
        pre_up = jnp.dot(rows_in, up_full, preferred_element_type=jnp.float32)
        back = lax.dot_general(grads_in, down_full, contract, preferred_element_type=jnp.float32)
        active, slope = silu_parts(pre_gate)
        gate_sum = jnp.sum(active * pre_up * back, axis=1)
        scaled = gate_values[expert][:, None] * back
        gate_delta = (scaled * pre_up * slope).astype(jnp.bfloat16)
        up_delta = (scaled * active).astype(jnp.bfloat16)
        gate_delta_blocks = gate_delta.reshape(CAP, blocks, ff_dev).transpose(1, 0, 2)
        up_delta_blocks = up_delta.reshape(CAP, blocks, ff_dev).transpose(1, 0, 2)
        gate_blocks = gate_full.reshape(D, blocks, ff_dev).transpose(1, 0, 2)
        up_blocks = up_full.reshape(D, blocks, ff_dev).transpose(1, 0, 2)

        def add_block(accum, pieces):
            delta_g, delta_u, weight_g, weight_u = pieces
            block_term = lax.dot_general(delta_g, weight_g, contract, preferred_element_type=jnp.float32)
            block_term = block_term + lax.dot_general(delta_u, weight_u, contract, preferred_element_type=jnp.float32)
            block_term = lax.optimization_barrier(block_term.astype(jnp.bfloat16)).astype(jnp.float32)
            return accum + block_term, None

        row_grads, _ = lax.scan(add_block, jnp.zeros((CAP, D), jnp.float32),
                                (gate_delta_blocks, up_delta_blocks, gate_blocks, up_blocks))
        total = total.at[rows].add(row_grads)
        table = table.at[expert].set(gate_sum)
        return (total, table), None

    start = (jnp.zeros((TOKENS, D), jnp.float32), jnp.zeros((EXPERTS, CAP), jnp.float32))
    (total, table), _ = lax.scan(per_expert, start, jnp.arange(EXPERTS, dtype=jnp.int32))
    return total.astype(jnp.bfloat16), table
```

```python
import jax
import jax.numpy as jnp
import numpy as np
from jax import lax
from jax.sharding import Mesh
from jax.sharding import PartitionSpec as P

NY, NZ, NX, NC = 8, 8, 4, 2
SLOTS = 8
BF = jnp.bfloat16
F32 = jnp.float32


def silu_parts(values):
    sig = jax.nn.sigmoid(values)
    return (values * sig, sig * (1.0 + values * (1.0 - sig)))


def swap_cores(a):
    return lax.ppermute(a, "c", [(0, 1), (1, 0)])


def shift_x(a, k):
    return lax.ppermute(a, "x", [(j, (j + k) % NX) for j in range(NX)])


def hi_lo(values):
    hi = values.astype(BF)
    lo = (values - hi.astype(F32)).astype(BF)
    return hi, lo


def on_device(tokens, output_grad, gate_weight, up_weight, down_weight, chosen, gate_values):
    expert = lax.axis_index("y")
    exp_index = expert * NZ + lax.axis_index("z")
    x_index = lax.axis_index("x")
    c_index = lax.axis_index("c")
    expert_count, capacity = chosen.shape
    token_rows, feat = tokens.shape
    hid = gate_weight.shape[2]
    peers = NY * NZ
    all_slots = peers * SLOTS
    wide = NC * feat

    source = chosen // token_rows
    local_rows = chosen - exp_index * token_rows
    mine = source == exp_index
    order = jnp.arange(capacity, dtype=jnp.int32)
    earlier = (order[:, None] < order[None, :]).astype(BF)
    rank = jnp.dot(mine.astype(BF), earlier, preferred_element_type=F32).astype(jnp.int32)
    slot_ids = jnp.arange(SLOTS, dtype=jnp.int32)
    hit = mine[:, None, :] & (rank[:, None, :] == slot_ids[None, :, None])
    send_row = jnp.sum(jnp.where(hit, local_rows[:, None, :] + 1, 0), axis=2) - 1
    token_ids = jnp.arange(token_rows, dtype=jnp.int32)
    pick = (send_row.reshape(-1)[:, None] == token_ids[None, :]).astype(BF)
    both = jnp.concatenate([tokens, output_grad], axis=1)
    picked = jnp.dot(pick, both, preferred_element_type=F32).astype(BF)
    outgoing = jnp.broadcast_to(
        picked.reshape(expert_count, 1, SLOTS, 2 * feat), (expert_count, NZ, SLOTS, 2 * feat)
    ).reshape(all_slots, 2 * feat)
    got = lax.all_to_all(outgoing, ("y", "z"), split_axis=0, concat_axis=0, tiled=True)

    gate_local = gate_weight[0]
    up_local = up_weight[0]
    down_local = down_weight[0]
    gu_all = jnp.zeros((NX, wide, 2 * hid), BF)
    down_all = jnp.zeros((NX, hid, wide), BF)
    for k in (1, 3, 2, 0):
        dest = (x_index + k) % NX
        g = lax.dynamic_slice_in_dim(gate_local, dest * wide, wide, 0)
        u = lax.dynamic_slice_in_dim(up_local, dest * wide, wide, 0)
        d = lax.dynamic_slice_in_dim(down_local, dest * wide, wide, 1)
        gu = jnp.concatenate([g, u], axis=1)
        if k:
            gu, d = shift_x(gu, k), shift_x(d, k)
        origin = (x_index - k) % NX
        gu_all = lax.dynamic_update_slice_in_dim(gu_all, gu[None], origin, 0)
        down_all = lax.dynamic_update_slice_in_dim(down_all, d[None], origin, 0)
    gu_cat = gu_all.transpose(1, 0, 2).reshape(wide, NX * 2 * hid)
    down_cat = down_all.reshape(NX * hid, wide)

    my_source = lax.dynamic_index_in_dim(source, expert, 0, keepdims=False)
    my_gates = lax.dynamic_index_in_dim(gate_values, expert, 0, keepdims=False)
    same = (my_source[:, None] == my_source[None, :]) & (order[None, :] < order[:, None])
    my_rank = jnp.sum(same.astype(jnp.int32), axis=1)
    my_slot = my_source * SLOTS + my_rank
    place = (my_slot[:, None] == jnp.arange(all_slots, dtype=jnp.int32)[None, :]).astype(BF)
    own = jnp.dot(place, got, preferred_element_type=F32).astype(BF)
    other = swap_cores(own)
    first = c_index == 0
    low, high = jnp.where(first, own, other), jnp.where(first, other, own)
    rows_in = jnp.concatenate([low[:, :feat], high[:, :feat]], axis=1)
    grads_in = jnp.concatenate([low[:, feat:], high[:, feat:]], axis=1)

    contract = (((1,), (1,)), ((), ()))
    pre_gu = jnp.dot(rows_in, gu_cat, preferred_element_type=F32).astype(BF)
    back = lax.dot_general(grads_in, down_cat, contract, preferred_element_type=F32).astype(BF)
    parts = jnp.stack(
        [
            jnp.concatenate(
                [pre_gu[:, j * 2 * hid : (j + 1) * 2 * hid], back[:, j * hid : (j + 1) * hid]], axis=1
            )
            for j in range(NX)
        ]
    )
    parts = lax.all_to_all(parts, "x", split_axis=0, concat_axis=0, tiled=True)
    sums = jnp.sum(parts.astype(F32), axis=0)
    pre_gate, pre_up, back = sums[:, :hid], sums[:, hid : 2 * hid], sums[:, 2 * hid :]
    active, slope = silu_parts(pre_gate)
    gate_part = jnp.sum(active * pre_up * back, axis=1)
    scaled = my_gates[:, None] * back
    gate_delta = (scaled * pre_up * slope).astype(BF)
    up_delta = (scaled * active).astype(BF)
    hi, lo = hi_lo(gate_part)
    extra = jnp.concatenate([hi, lo, jnp.zeros((16 * 2 * hid - 2 * capacity,), BF)]).reshape(16, 2 * hid)
    deltas = jnp.concatenate([jnp.concatenate([gate_delta, up_delta], axis=1), extra], axis=0)
    deltas = lax.all_gather(deltas, "x", axis=0, tiled=False)
    gate_rows = deltas[:, capacity:].reshape(NX, -1).astype(F32)
    gate_sum = jnp.sum(gate_rows[:, :capacity] + gate_rows[:, capacity : 2 * capacity], axis=0)
    delta_cat = deltas[:, :capacity].transpose(1, 0, 2).reshape(capacity, NX * 2 * hid)
    term = lax.dot_general(delta_cat, gu_cat, contract, preferred_element_type=F32)
    hi, lo = hi_lo(gate_sum)
    extra = jnp.concatenate([hi, lo, jnp.zeros((16 * feat - 2 * capacity,), BF)]).reshape(16, feat)
    keep, give = jnp.where(first, term[:, :feat], term[:, feat:]), jnp.where(first, term[:, feat:], term[:, :feat])
    came = swap_cores(jnp.concatenate([give.astype(BF), extra], axis=0))
    term = (keep + came[:capacity].astype(F32)).astype(BF)
    came_gate = came[capacity:].reshape(-1).astype(F32)
    gate_sum = (hi.astype(F32) + lo.astype(F32)) + (came_gate[:capacity] + came_gate[capacity : 2 * capacity])
    hi, lo = hi_lo(gate_sum)
    gate_block = jnp.concatenate([hi, lo, jnp.zeros((SLOTS * 128 - 2 * capacity,), BF)]).reshape(1, SLOTS, 128)
    gate_block = jnp.broadcast_to(gate_block, (peers, SLOTS, 128)).reshape(all_slots, 128)
    spread = lax.dot_general(place, term, (((0,), (0,)), ((), ())), preferred_element_type=F32).astype(BF)
    home = lax.all_to_all(
        jnp.concatenate([spread, gate_block], axis=1), ("y", "z"), split_axis=0, concat_axis=0, tiled=True
    )
    owner = jnp.broadcast_to(
        pick.reshape(expert_count, 1, SLOTS, token_rows), (expert_count, NZ, SLOTS, token_rows)
    ).reshape(all_slots, token_rows)
    grad_tokens = lax.dot_general(
        owner, home[:, :feat], (((0,), (0,)), ((), ())), preferred_element_type=F32
    ).astype(BF)
    gates = jnp.sum(home[:, feat:].reshape(expert_count, NZ, SLOTS * 128).astype(F32), axis=1)
    gate_grad = gates[:, :capacity] + gates[:, capacity : 2 * capacity]
    return grad_tokens, gate_grad


def solution(mesh):
    grid = Mesh(np.asarray(mesh.devices).reshape(NY, NZ, NX, NC), ("y", "z", "x", "c"))
    exp, ten = ("y", "z"), ("x", "c")
    in_specs = (
        P(exp, ten),
        P(exp, ten),
        P(exp, None, ten),
        P(exp, None, ten),
        P(exp, ten, None),
        P(),
        P(),
    )
    out_specs = (P(exp, ten), P())
    return jax.shard_map(on_device, mesh=grid, in_specs=in_specs, out_specs=out_specs, check_vma=False)
```

```python
import jax
import jax.numpy as jnp
import numpy as np
from jax import lax
from jax.experimental import pallas as pl
from jax.experimental.pallas import tpu as pltpu
from jax.sharding import Mesh
from jax.sharding import PartitionSpec as P

NY, NZ, NX, NC = 8, 8, 4, 2
SLOTS = 8
BF = jnp.bfloat16
F32 = jnp.float32
VMEM = 12 * 1024 * 1024
CONTRACT = (((1,), (1,)), ((), ()))


def silu_parts(values):
    sig = jax.nn.sigmoid(values)
    return (values * sig, sig * (1.0 + values * (1.0 - sig)))


def swap_cores(a):
    return lax.ppermute(a, "c", [(0, 1), (1, 0)])


def shift_x(a, k):
    return lax.ppermute(a, "x", [(j, (j + k) % NX) for j in range(NX)])


def hi_lo(values):
    hi = values.astype(BF)
    lo = (values - hi.astype(F32)).astype(BF)
    return hi, lo


def pack_kernel(where_ref, gate_ref, up_ref, down_ref, out_ref, sems):
    hid = gate_ref.shape[1]
    half = out_ref.shape[0] // 3
    chunk = out_ref.shape[1]
    copies = []
    for h in range(NC):
        start = pl.multiple_of(where_ref[h], half)
        rows = pl.ds(h * half, half)
        copies.append((gate_ref.at[pl.ds(start, half), :], out_ref.at[rows, pl.ds(0, hid)]))
        copies.append((up_ref.at[pl.ds(start, half), :], out_ref.at[rows, pl.ds(hid, hid)]))
        for q in range(half // chunk):
            begin = pl.multiple_of(start + q * chunk, chunk)
            low = NC * half + (h * (half // chunk) + q) * hid
            copies.append((down_ref.at[:, pl.ds(begin, chunk)], out_ref.at[pl.ds(low, hid), :]))
    started = []
    for i, (src, dst) in enumerate(copies):
        copy = pltpu.make_async_copy(src, dst, sems.at[i])
        copy.start()
        started.append(copy)
    for copy in started:
        copy.wait()


def pack(gate, up, down, where, feat):
    hid = gate.shape[1]
    chunk = 2 * hid
    rows = NC * feat + NC * (feat // chunk) * hid
    n = NC * (2 + feat // chunk)
    anywhere = pl.BlockSpec(memory_space=pltpu.HBM)
    return pl.pallas_call(
        pack_kernel,
        out_shape=jax.ShapeDtypeStruct((rows, chunk), BF),
        in_specs=[pl.BlockSpec(memory_space=pltpu.SMEM), anywhere, anywhere, anywhere],
        scratch_shapes=[pltpu.SemaphoreType.DMA((n,))],
        compiler_params=pltpu.CompilerParams(vmem_limit_bytes=VMEM),
        name="pack_weights",
    )(where, gate, up, down)


def pre_kernel(own_ref, other_ref, w_ref, out_ref):
    feat = own_ref.shape[1] // 2
    chunk = w_ref.shape[1]
    hid = chunk // 2
    gu = None
    back = None
    for h, rows in enumerate((own_ref, other_ref)):
        term = jnp.dot(rows[:, :feat], w_ref[h * feat : (h + 1) * feat, :], preferred_element_type=F32)
        gu = term if gu is None else gu + term
        for q in range(feat // chunk):
            low = NC * feat + (h * (feat // chunk) + q) * hid
            term = lax.dot_general(
                rows[:, feat + q * chunk : feat + (q + 1) * chunk],
                w_ref[low : low + hid, :],
                CONTRACT,
                preferred_element_type=F32,
            )
            back = term if back is None else back + term
    out_ref[:, :chunk] = gu.astype(BF)
    out_ref[:, chunk:] = back.astype(BF)


def pre_part(own, other, w):
    rows = own.shape[0]
    return pl.pallas_call(
        pre_kernel,
        out_shape=jax.ShapeDtypeStruct((rows, w.shape[1] // 2 * 3), BF),
        compiler_params=pltpu.CompilerParams(vmem_limit_bytes=VMEM),
        name="pre_part",
    )(own, other, w)


def give_kernel(from_ref, d_ref, w0, w1, w2, w3, extra_ref, give_ref, keep_ref):
    rows, feat = keep_ref.shape
    for h in (1, 0):
        total = None
        for k, w in enumerate((w0, w1, w2, w3)):
            term = lax.dot_general(
                d_ref[from_ref[k], :rows, :],
                w[h * feat : (h + 1) * feat, :],
                CONTRACT,
                preferred_element_type=F32,
            )
            total = term if total is None else total + term
        if h:
            give_ref[:rows, :] = total.astype(BF)
            give_ref[rows:, :] = extra_ref[...]
        else:
            keep_ref[...] = total


def give_keep(origin, deltas, weights, extra, rows, feat):
    vmem = pl.BlockSpec(memory_space=pltpu.VMEM)
    return pl.pallas_call(
        give_kernel,
        out_shape=(
            jax.ShapeDtypeStruct((rows + extra.shape[0], feat), BF),
            jax.ShapeDtypeStruct((rows, feat), F32),
        ),
        in_specs=[pl.BlockSpec(memory_space=pltpu.SMEM)] + [vmem] * 6,
        compiler_params=pltpu.CompilerParams(vmem_limit_bytes=VMEM),
        name="input_grads",
    )(origin, deltas, *weights, extra)


def spread_kernel(keep_ref, came_ref, place_ref, gate_ref, out_ref):
    rows, feat = keep_ref.shape
    term = (keep_ref[...] + came_ref[:rows, :].astype(F32)).astype(BF)
    out_ref[:, :feat] = jnp.dot(place_ref[...], term, preferred_element_type=F32).astype(BF)
    block = gate_ref[...]
    slots = out_ref.shape[0]
    block = jnp.broadcast_to(block[None], (slots // SLOTS, SLOTS, 128)).reshape(slots, 128)
    out_ref[:, feat:] = block.astype(BF)


def spread_out(keep, came, place_t, gate_block):
    slots, feat = place_t.shape[0], keep.shape[1]
    return pl.pallas_call(
        spread_kernel,
        out_shape=jax.ShapeDtypeStruct((slots, feat + 128), BF),
        compiler_params=pltpu.CompilerParams(vmem_limit_bytes=VMEM),
        name="rows_to_slots",
    )(keep, came, place_t, gate_block)


def on_device(tokens, output_grad, gate_weight, up_weight, down_weight, chosen, gate_values):
    expert = lax.axis_index("y")
    exp_index = expert * NZ + lax.axis_index("z")
    x_index = lax.axis_index("x")
    c_index = lax.axis_index("c")
    expert_count, capacity = chosen.shape
    token_rows, feat = tokens.shape
    hid = gate_weight.shape[2]
    peers = NY * NZ
    all_slots = peers * SLOTS
    wide = NC * feat

    packed = {}
    for k in (2, 1, 3, 0):
        dest = (x_index + k) % NX
        where = jnp.stack([dest * wide + c_index * feat, dest * wide + (1 - c_index) * feat])
        packed[k] = pack(gate_weight[0], up_weight[0], down_weight[0], where, feat)
    weights = {0: packed[0]}
    for k in (2, 1, 3):
        weights[k] = shift_x(packed[k], k)

    source = chosen // token_rows
    local_rows = chosen - exp_index * token_rows
    mine = source == exp_index
    order = jnp.arange(capacity, dtype=jnp.int32)
    earlier = (order[:, None] < order[None, :]).astype(BF)
    rank = jnp.dot(mine.astype(BF), earlier, preferred_element_type=F32).astype(jnp.int32)
    slot_ids = jnp.arange(SLOTS, dtype=jnp.int32)
    hit = mine[:, None, :] & (rank[:, None, :] == slot_ids[None, :, None])
    send_row = jnp.sum(jnp.where(hit, local_rows[:, None, :] + 1, 0), axis=2) - 1
    token_ids = jnp.arange(token_rows, dtype=jnp.int32)
    pick = (send_row.reshape(-1)[:, None] == token_ids[None, :]).astype(BF)
    both = jnp.concatenate([tokens, output_grad], axis=1)
    picked = jnp.dot(pick, both, preferred_element_type=F32).astype(BF)
    outgoing = jnp.broadcast_to(
        picked.reshape(expert_count, 1, SLOTS, 2 * feat), (expert_count, NZ, SLOTS, 2 * feat)
    ).reshape(all_slots, 2 * feat)
    got = lax.all_to_all(outgoing, ("y", "z"), split_axis=0, concat_axis=0, tiled=True)
    got, weights[2], weights[1] = lax.optimization_barrier((got, weights[2], weights[1]))

    my_source = lax.dynamic_index_in_dim(source, expert, 0, keepdims=False)
    my_gates = lax.dynamic_index_in_dim(gate_values, expert, 0, keepdims=False)
    same = (my_source[:, None] == my_source[None, :]) & (order[None, :] < order[:, None])
    my_rank = jnp.sum(same.astype(jnp.int32), axis=1)
    my_slot = my_source * SLOTS + my_rank
    slot_order = jnp.arange(all_slots, dtype=jnp.int32)
    place = (my_slot[:, None] == slot_order[None, :]).astype(BF)
    place_t = (my_slot[None, :] == slot_order[:, None]).astype(BF)
    own = jnp.dot(place, got, preferred_element_type=F32).astype(BF)
    other = swap_cores(own)
    other, weights[3] = lax.optimization_barrier((other, weights[3]))

    sums = None
    for k in (2, 1, 3, 0):
        part = pre_part(own, other, weights[(NX - k) % NX])
        part = (shift_x(part, k) if k else part).astype(F32)
        sums = part if sums is None else sums + part
    pre_gate, pre_up, back = sums[:, :hid], sums[:, hid : 2 * hid], sums[:, 2 * hid :]
    active, slope = silu_parts(pre_gate)
    gate_part = jnp.sum(active * pre_up * back, axis=1)
    scaled = my_gates[:, None] * back
    gate_delta = (scaled * pre_up * slope).astype(BF)
    up_delta = (scaled * active).astype(BF)
    hi, lo = hi_lo(gate_part)
    extra = jnp.concatenate([hi, lo, jnp.zeros((16 * 2 * hid - 2 * capacity,), BF)]).reshape(16, 2 * hid)
    delta = jnp.concatenate([jnp.concatenate([gate_delta, up_delta], axis=1), extra], axis=0)
    deltas = lax.all_gather(delta, "x", axis=0, tiled=False)
    gate_rows = deltas[:, capacity:].reshape(NX, -1).astype(F32)
    gate_sum = jnp.sum(gate_rows[:, :capacity] + gate_rows[:, capacity : 2 * capacity], axis=0)
    origin = (x_index - jnp.arange(NX, dtype=jnp.int32)) % NX
    hi, lo = hi_lo(gate_sum)
    extra = jnp.concatenate([hi, lo, jnp.zeros((16 * feat - 2 * capacity,), BF)]).reshape(16, feat)
    give, keep = give_keep(
        origin, deltas, [weights[k] for k in range(NX)], extra, capacity, feat
    )
    came = swap_cores(give)
    came_gate = came[capacity:].reshape(-1).astype(F32)
    gate_sum = (hi.astype(F32) + lo.astype(F32)) + (came_gate[:capacity] + came_gate[capacity : 2 * capacity])
    hi, lo = hi_lo(gate_sum)
    gate_block = jnp.concatenate([hi, lo, jnp.zeros((SLOTS * 128 - 2 * capacity,), BF)])
    gate_block = gate_block.astype(F32).reshape(SLOTS, 128)
    home = lax.all_to_all(
        spread_out(keep, came, place_t, gate_block), ("y", "z"), split_axis=0, concat_axis=0, tiled=True
    )
    owner = jnp.broadcast_to(
        pick.reshape(expert_count, 1, SLOTS, token_rows), (expert_count, NZ, SLOTS, token_rows)
    ).reshape(all_slots, token_rows)
    grad_tokens = lax.dot_general(
        owner, home[:, :feat], (((0,), (0,)), ((), ())), preferred_element_type=F32
    ).astype(BF)
    gates = jnp.sum(home[:, feat:].reshape(expert_count, NZ, SLOTS * 128).astype(F32), axis=1)
    gate_grad = gates[:, :capacity] + gates[:, capacity : 2 * capacity]
    return grad_tokens, gate_grad


def solution(mesh):
    grid = Mesh(np.asarray(mesh.devices).reshape(NY, NZ, NX, NC), ("y", "z", "x", "c"))
    exp, ten = ("y", "z"), ("x", "c")
    in_specs = (
        P(exp, ten),
        P(exp, ten),
        P(exp, None, ten),
        P(exp, None, ten),
        P(exp, ten, None),
        P(),
        P(),
    )
    out_specs = (P(exp, ten), P())
    return jax.shard_map(on_device, mesh=grid, in_specs=in_specs, out_specs=out_specs, check_vma=False)
```

```python
import jax
import jax.numpy as jnp
import numpy as np
from jax import lax
from jax.experimental import pallas as pl
from jax.experimental.pallas import tpu as pltpu
from jax.sharding import Mesh
from jax.sharding import PartitionSpec as P

NY, NZ, NX, NC = 8, 8, 4, 2
SLOTS = 8
BF = jnp.bfloat16
F32 = jnp.float32
VMEM = 12 * 1024 * 1024
CONTRACT = (((1,), (1,)), ((), ()))


def silu_parts(values):
    sig = jax.nn.sigmoid(values)
    return (values * sig, sig * (1.0 + values * (1.0 - sig)))


def swap_cores(a):
    return lax.ppermute(a, "c", [(0, 1), (1, 0)])


def shift_x(a, k):
    return lax.ppermute(a, "x", [(j, (j + k) % NX) for j in range(NX)])


def hi_lo(values):
    hi = values.astype(BF)
    lo = (values - hi.astype(F32)).astype(BF)
    return hi, lo


def prologue_kernel(
    where_ref, chosen_ref, tokens_ref, grads_ref, gate_ref, up_ref, down_ref,
    out0, out1, out2, out3, rows_ref, pick_ref, sems,
):
    hid = gate_ref.shape[1]
    token_rows, feat = tokens_ref.shape
    chunk = 2 * hid
    outs = (out0, out1, out2, out3)
    started = []
    for k in (1, 3, 2, 0):
        for h in range(NC):
            start = pl.multiple_of(where_ref[k * NC + h], feat)
            rows = pl.ds(h * feat, feat)
            copies = [
                (gate_ref.at[pl.ds(start, feat), :], outs[k].at[rows, pl.ds(0, hid)]),
                (up_ref.at[pl.ds(start, feat), :], outs[k].at[rows, pl.ds(hid, hid)]),
            ]
            for q in range(feat // chunk):
                begin = pl.multiple_of(start + q * chunk, chunk)
                low = NC * feat + (h * (feat // chunk) + q) * hid
                copies.append((down_ref.at[:, pl.ds(begin, chunk)], outs[k].at[pl.ds(low, hid), :]))
            for src, dst in copies:
                copy = pltpu.make_async_copy(src, dst, sems.at[len(started)])
                copy.start()
                started.append(copy)
    experts, capacity = chosen_ref.shape
    local = chosen_ref[...] - where_ref[NX * NC]
    mine = (local >= 0) & (local < token_rows)
    earlier = lax.broadcasted_iota(jnp.int32, (capacity, capacity), 0) < lax.broadcasted_iota(
        jnp.int32, (capacity, capacity), 1
    )
    earlier = jnp.where(earlier, 1.0, 0.0).astype(BF)
    rank = jnp.dot(jnp.where(mine, 1.0, 0.0).astype(BF), earlier, preferred_element_type=F32)
    key = jnp.where(mine, (local + 1).astype(F32), 0.0)
    slot = lax.broadcasted_iota(jnp.int32, (SLOTS, capacity), 0).astype(F32)
    token = lax.broadcasted_iota(jnp.int32, (SLOTS, token_rows), 1).astype(F32) + 1.0
    picks = []
    for e in range(experts):
        hit = slot == jnp.broadcast_to(rank[e : e + 1, :], slot.shape)
        row = jnp.sum(jnp.where(hit, jnp.broadcast_to(key[e : e + 1, :], slot.shape), 0.0), axis=1, keepdims=True)
        picks.append(jnp.where(row == token, 1.0, 0.0))
    pick = jnp.concatenate(picks, axis=0).astype(BF)
    pick_ref[...] = pick
    for i, ref in enumerate((tokens_ref, grads_ref)):
        picked = jnp.dot(pick, ref[...], preferred_element_type=F32)
        picked = picked.reshape(experts, 1, SLOTS, feat)
        picked = jnp.broadcast_to(picked, (experts, NZ, SLOTS, feat)).reshape(experts * NZ * SLOTS, feat)
        rows_ref[:, i * feat : (i + 1) * feat] = picked.astype(BF)
    for copy in started:
        copy.wait()


def prologue(where, chosen, tokens, grads, gate, up, down):
    token_rows, feat = tokens.shape
    hid = gate.shape[1]
    chunk = 2 * hid
    packed = jax.ShapeDtypeStruct((NC * feat + NC * (feat // chunk) * hid, chunk), BF)
    n = NX * NC * (2 + feat // chunk)
    picks = chosen.shape[0] * SLOTS
    hbm = pl.BlockSpec(memory_space=pltpu.HBM)
    vmem = pl.BlockSpec(memory_space=pltpu.VMEM)
    return pl.pallas_call(
        prologue_kernel,
        out_shape=(
            packed, packed, packed, packed,
            jax.ShapeDtypeStruct((picks * NZ, 2 * feat), BF),
            jax.ShapeDtypeStruct((picks, token_rows), BF),
        ),
        in_specs=[pl.BlockSpec(memory_space=pltpu.SMEM), vmem, vmem, vmem, hbm, hbm, hbm],
        scratch_shapes=[pltpu.SemaphoreType.DMA((n,))],
        compiler_params=pltpu.CompilerParams(vmem_limit_bytes=60 * 1024 * 1024),
        name="prologue",
    )(where, chosen, tokens, grads, gate, up, down)


def pre_kernel(own_ref, other_ref, w_ref, out_ref):
    feat = own_ref.shape[1] // 2
    chunk = w_ref.shape[1]
    hid = chunk // 2
    gu = None
    back = None
    for h, rows in enumerate((own_ref, other_ref)):
        term = jnp.dot(rows[:, :feat], w_ref[h * feat : (h + 1) * feat, :], preferred_element_type=F32)
        gu = term if gu is None else gu + term
        for q in range(feat // chunk):
            low = NC * feat + (h * (feat // chunk) + q) * hid
            term = lax.dot_general(
                rows[:, feat + q * chunk : feat + (q + 1) * chunk],
                w_ref[low : low + hid, :],
                CONTRACT,
                preferred_element_type=F32,
            )
            back = term if back is None else back + term
    out_ref[:, :chunk] = gu.astype(BF)
    out_ref[:, chunk:] = back.astype(BF)


def pre_part(own, other, w):
    rows = own.shape[0]
    return pl.pallas_call(
        pre_kernel,
        out_shape=jax.ShapeDtypeStruct((rows, w.shape[1] // 2 * 3), BF),
        compiler_params=pltpu.CompilerParams(vmem_limit_bytes=VMEM),
        name="pre_part",
    )(own, other, w)


def give_kernel(from_ref, d_ref, w0, w1, w2, w3, extra_ref, give_ref, keep_ref):
    rows, feat = keep_ref.shape
    for h in (1, 0):
        total = None
        for k, w in enumerate((w0, w1, w2, w3)):
            term = lax.dot_general(
                d_ref[from_ref[k], :rows, :],
                w[h * feat : (h + 1) * feat, :],
                CONTRACT,
                preferred_element_type=F32,
            )
            total = term if total is None else total + term
        if h:
            give_ref[:rows, :] = total.astype(BF)
            give_ref[rows:, :] = extra_ref[...]
        else:
            keep_ref[...] = total


def give_keep(origin, deltas, weights, extra, rows, feat):
    vmem = pl.BlockSpec(memory_space=pltpu.VMEM)
    return pl.pallas_call(
        give_kernel,
        out_shape=(
            jax.ShapeDtypeStruct((rows + extra.shape[0], feat), BF),
            jax.ShapeDtypeStruct((rows, feat), F32),
        ),
        in_specs=[pl.BlockSpec(memory_space=pltpu.SMEM)] + [vmem] * 6,
        compiler_params=pltpu.CompilerParams(vmem_limit_bytes=VMEM),
        name="input_grads",
    )(origin, deltas, *weights, extra)


def spread_kernel(keep_ref, came_ref, place_ref, gate_ref, out_ref):
    rows, feat = keep_ref.shape
    term = (keep_ref[...] + came_ref[:rows, :].astype(F32)).astype(BF)
    out_ref[:, :feat] = jnp.dot(place_ref[...], term, preferred_element_type=F32).astype(BF)
    block = gate_ref[...]
    slots = out_ref.shape[0]
    block = jnp.broadcast_to(block[None], (slots // SLOTS, SLOTS, 128)).reshape(slots, 128)
    out_ref[:, feat:] = block.astype(BF)


def spread_out(keep, came, place_t, gate_block):
    slots, feat = place_t.shape[0], keep.shape[1]
    return pl.pallas_call(
        spread_kernel,
        out_shape=jax.ShapeDtypeStruct((slots, feat + 128), BF),
        compiler_params=pltpu.CompilerParams(vmem_limit_bytes=VMEM),
        name="rows_to_slots",
    )(keep, came, place_t, gate_block)


def on_device(tokens, output_grad, gate_weight, up_weight, down_weight, chosen, gate_values):
    expert = lax.axis_index("y")
    exp_index = expert * NZ + lax.axis_index("z")
    x_index = lax.axis_index("x")
    c_index = lax.axis_index("c")
    expert_count, capacity = chosen.shape
    token_rows, feat = tokens.shape
    hid = gate_weight.shape[2]
    peers = NY * NZ
    all_slots = peers * SLOTS
    wide = NC * feat

    dest = (x_index + jnp.arange(NX, dtype=jnp.int32)) % NX * wide
    where = jnp.stack([dest + c_index * feat, dest + (1 - c_index) * feat], axis=1).reshape(-1)
    where = jnp.concatenate([where, (exp_index * token_rows)[None]]).astype(jnp.int32)
    *packed, outgoing, pick = prologue(
        where, chosen, tokens, output_grad, gate_weight[0], up_weight[0], down_weight[0]
    )
    weights = {0: packed[0]}
    for k in (1, 3, 2):
        weights[k] = shift_x(packed[k], k)
    got = lax.all_to_all(outgoing, ("y", "z"), split_axis=0, concat_axis=0, tiled=True)
    got, weights[1] = lax.optimization_barrier((got, weights[1]))

    source = chosen // token_rows
    order = jnp.arange(capacity, dtype=jnp.int32)
    my_source = lax.dynamic_index_in_dim(source, expert, 0, keepdims=False)
    my_gates = lax.dynamic_index_in_dim(gate_values, expert, 0, keepdims=False)
    same = (my_source[:, None] == my_source[None, :]) & (order[None, :] < order[:, None])
    my_rank = jnp.sum(same.astype(jnp.int32), axis=1)
    my_slot = my_source * SLOTS + my_rank
    slot_order = jnp.arange(all_slots, dtype=jnp.int32)
    place = (my_slot[:, None] == slot_order[None, :]).astype(BF)
    place_t = (my_slot[None, :] == slot_order[:, None]).astype(BF)
    own = jnp.dot(place, got, preferred_element_type=F32).astype(BF)
    other = swap_cores(own)
    other, weights[3], weights[2] = lax.optimization_barrier((other, weights[3], weights[2]))
    sums = None
    for k in (1, 3, 0, 2):
        part = pre_part(own, other, weights[(NX - k) % NX])
        part = (shift_x(part, k) if k else part).astype(F32)
        sums = part if sums is None else sums + part
    pre_gate, pre_up, back = sums[:, :hid], sums[:, hid : 2 * hid], sums[:, 2 * hid :]
    active, slope = silu_parts(pre_gate)
    gate_part = jnp.sum(active * pre_up * back, axis=1)
    scaled = my_gates[:, None] * back
    gate_delta = (scaled * pre_up * slope).astype(BF)
    up_delta = (scaled * active).astype(BF)
    hi, lo = hi_lo(gate_part)
    extra = jnp.concatenate([hi, lo, jnp.zeros((16 * 2 * hid - 2 * capacity,), BF)]).reshape(16, 2 * hid)
    delta = jnp.concatenate([jnp.concatenate([gate_delta, up_delta], axis=1), extra], axis=0)
    deltas = lax.all_gather(delta, "x", axis=0, tiled=False)
    gate_rows = deltas[:, capacity:].reshape(NX, -1).astype(F32)
    gate_sum = jnp.sum(gate_rows[:, :capacity] + gate_rows[:, capacity : 2 * capacity], axis=0)
    origin = (x_index - jnp.arange(NX, dtype=jnp.int32)) % NX
    hi, lo = hi_lo(gate_sum)
    extra = jnp.concatenate([hi, lo, jnp.zeros((16 * feat - 2 * capacity,), BF)]).reshape(16, feat)
    give, keep = give_keep(
        origin, deltas, [weights[k] for k in range(NX)], extra, capacity, feat
    )
    came = swap_cores(give)
    came_gate = came[capacity:].reshape(-1).astype(F32)
    gate_sum = (hi.astype(F32) + lo.astype(F32)) + (came_gate[:capacity] + came_gate[capacity : 2 * capacity])
    hi, lo = hi_lo(gate_sum)
    gate_block = jnp.concatenate([hi, lo, jnp.zeros((SLOTS * 128 - 2 * capacity,), BF)])
    gate_block = gate_block.astype(F32).reshape(SLOTS, 128)
    home = lax.all_to_all(
        spread_out(keep, came, place_t, gate_block), ("y", "z"), split_axis=0, concat_axis=0, tiled=True
    )
    owner = jnp.broadcast_to(
        pick.reshape(expert_count, 1, SLOTS, token_rows), (expert_count, NZ, SLOTS, token_rows)
    ).reshape(all_slots, token_rows)
    grad_tokens = lax.dot_general(
        owner, home[:, :feat], (((0,), (0,)), ((), ())), preferred_element_type=F32
    ).astype(BF)
    gates = jnp.sum(home[:, feat:].reshape(expert_count, NZ, SLOTS * 128).astype(F32), axis=1)
    gate_grad = gates[:, :capacity] + gates[:, capacity : 2 * capacity]
    return grad_tokens, gate_grad


def solution(mesh):
    grid = Mesh(np.asarray(mesh.devices).reshape(NY, NZ, NX, NC), ("y", "z", "x", "c"))
    exp, ten = ("y", "z"), ("x", "c")
    in_specs = (
        P(exp, ten),
        P(exp, ten),
        P(exp, None, ten),
        P(exp, None, ten),
        P(exp, ten, None),
        P(),
        P(),
    )
    out_specs = (P(exp, ten), P())
    return jax.shard_map(on_device, mesh=grid, in_specs=in_specs, out_specs=out_specs, check_vma=False)
```

```python
import jax
import jax.numpy as jnp
import numpy as np
from jax import lax
from jax.experimental import pallas as pl
from jax.experimental.pallas import tpu as pltpu
from jax.sharding import Mesh
from jax.sharding import PartitionSpec as P

NY, NZ, NX, NC = 8, 8, 4, 2
SLOTS = 8
BF = jnp.bfloat16
F32 = jnp.float32
VMEM = 12 * 1024 * 1024
BIG_VMEM = 60 * 1024 * 1024
CONTRACT = (((1,), (1,)), ((), ()))


def silu_parts(values):
    sig = jax.nn.sigmoid(values)
    return (values * sig, sig * (1.0 + values * (1.0 - sig)))


def swap_cores(a):
    return lax.ppermute(a, "c", [(0, 1), (1, 0)])


def shift_x(a, k):
    return lax.ppermute(a, "x", [(j, (j + k) % NX) for j in range(NX)])


def hi_lo(values):
    hi = values.astype(BF)
    lo = (values - hi.astype(F32)).astype(BF)
    return hi, lo


def start_packing(start_of, gate_ref, up_ref, down_ref, outs, sems):
    hid = gate_ref.shape[1]
    chunk = 2 * hid
    feat = outs[0].shape[0] // 3
    started = []
    for k, out in enumerate(outs):
        for h in range(NC):
            start = pl.multiple_of(start_of[k * NC + h], feat)
            rows = pl.ds(h * feat, feat)
            copies = [
                (gate_ref.at[pl.ds(start, feat), :], out.at[rows, pl.ds(0, hid)]),
                (up_ref.at[pl.ds(start, feat), :], out.at[rows, pl.ds(hid, hid)]),
            ]
            for q in range(feat // chunk):
                begin = pl.multiple_of(start + q * chunk, chunk)
                low = NC * feat + (h * (feat // chunk) + q) * hid
                copies.append((down_ref.at[:, pl.ds(begin, chunk)], out.at[pl.ds(low, hid), :]))
            for src, dst in copies:
                copy = pltpu.make_async_copy(src, dst, sems.at[len(started)])
                copy.start()
                started.append(copy)
    return started


def packed_shape(hid, feat):
    return jax.ShapeDtypeStruct((NC * feat + feat // 2 // hid * NC * hid, 2 * hid), BF)


def pack_copies(hid, feat, count):
    return pltpu.SemaphoreType.DMA((count * NC * (2 + feat // 2 // hid),))


def pack_kernel(where_ref, gate_ref, up_ref, down_ref, *refs):
    for copy in start_packing(where_ref, gate_ref, up_ref, down_ref, refs[:-1], refs[-1]):
        copy.wait()


def pack_weights(where, gate, up, down, feat, limit):
    hid = gate.shape[1]
    count = where.shape[0] // NC
    hbm = pl.BlockSpec(memory_space=pltpu.HBM)
    return pl.pallas_call(
        pack_kernel,
        out_shape=(packed_shape(hid, feat),) * count,
        in_specs=[pl.BlockSpec(memory_space=pltpu.SMEM), hbm, hbm, hbm],
        scratch_shapes=[pack_copies(hid, feat, count)],
        compiler_params=pltpu.CompilerParams(vmem_limit_bytes=limit),
        name="pack_weights",
    )(where, gate, up, down)


def pick_kernel(
    base_ref, chosen_ref, tokens_ref, grads_ref, gate_ref, up_ref, down_ref, rows_ref, pick_ref, out_ref, sems
):
    started = start_packing(base_ref, gate_ref, up_ref, down_ref, [out_ref], sems)
    token_rows, feat = tokens_ref.shape
    experts, capacity = chosen_ref.shape
    local = chosen_ref[...] - base_ref[NC]
    mine = (local >= 0) & (local < token_rows)
    earlier = lax.broadcasted_iota(jnp.int32, (capacity, capacity), 0) < lax.broadcasted_iota(
        jnp.int32, (capacity, capacity), 1
    )
    earlier = jnp.where(earlier, 1.0, 0.0).astype(BF)
    rank = jnp.dot(jnp.where(mine, 1.0, 0.0).astype(BF), earlier, preferred_element_type=F32)
    key = jnp.where(mine, (local + 1).astype(F32), 0.0)
    slot = lax.broadcasted_iota(jnp.int32, (SLOTS, capacity), 0).astype(F32)
    token = lax.broadcasted_iota(jnp.int32, (SLOTS, token_rows), 1).astype(F32) + 1.0
    picks = []
    for e in range(experts):
        hit = slot == jnp.broadcast_to(rank[e : e + 1, :], slot.shape)
        row = jnp.sum(jnp.where(hit, jnp.broadcast_to(key[e : e + 1, :], slot.shape), 0.0), axis=1, keepdims=True)
        picks.append(jnp.where(row == token, 1.0, 0.0))
    pick = jnp.concatenate(picks, axis=0).astype(BF)
    pick_ref[...] = pick
    for i, ref in enumerate((tokens_ref, grads_ref)):
        picked = jnp.dot(pick, ref[...], preferred_element_type=F32)
        picked = picked.reshape(experts, 1, SLOTS, feat)
        picked = jnp.broadcast_to(picked, (experts, NZ, SLOTS, feat)).reshape(experts * NZ * SLOTS, feat)
        rows_ref[:, i * feat : (i + 1) * feat] = picked.astype(BF)
    for copy in started:
        copy.wait()


def pick_rows(base, chosen, tokens, grads, gate, up, down):
    hid = gate.shape[1]
    hbm = pl.BlockSpec(memory_space=pltpu.HBM)
    token_rows, feat = tokens.shape
    picks = chosen.shape[0] * SLOTS
    vmem = pl.BlockSpec(memory_space=pltpu.VMEM)
    return pl.pallas_call(
        pick_kernel,
        out_shape=(
            jax.ShapeDtypeStruct((picks * NZ, 2 * feat), BF),
            jax.ShapeDtypeStruct((picks, token_rows), BF),
            packed_shape(hid, feat),
        ),
        in_specs=[pl.BlockSpec(memory_space=pltpu.SMEM), vmem, vmem, vmem, hbm, hbm, hbm],
        scratch_shapes=[pack_copies(hid, feat, 1)],
        compiler_params=pltpu.CompilerParams(vmem_limit_bytes=BIG_VMEM),
        name="pick_rows",
    )(base, chosen, tokens, grads, gate, up, down)


def pre_kernel(own_ref, other_ref, w_ref, out_ref):
    feat = own_ref.shape[1] // 2
    chunk = w_ref.shape[1]
    hid = chunk // 2
    gu = None
    back = None
    for h, rows in enumerate((own_ref, other_ref)):
        term = jnp.dot(rows[:, :feat], w_ref[h * feat : (h + 1) * feat, :], preferred_element_type=F32)
        gu = term if gu is None else gu + term
        for q in range(feat // chunk):
            low = NC * feat + (h * (feat // chunk) + q) * hid
            term = lax.dot_general(
                rows[:, feat + q * chunk : feat + (q + 1) * chunk],
                w_ref[low : low + hid, :],
                CONTRACT,
                preferred_element_type=F32,
            )
            back = term if back is None else back + term
    out_ref[:, :chunk] = gu.astype(BF)
    out_ref[:, chunk:] = back.astype(BF)


def pre_part(own, other, w):
    rows = own.shape[0]
    return pl.pallas_call(
        pre_kernel,
        out_shape=jax.ShapeDtypeStruct((rows, w.shape[1] // 2 * 3), BF),
        compiler_params=pltpu.CompilerParams(vmem_limit_bytes=VMEM),
        name="pre_part",
    )(own, other, w)


def give_kernel(from_ref, d_ref, w0, w1, w2, w3, extra_ref, give_ref, keep_ref):
    rows, feat = keep_ref.shape
    for h in (1, 0):
        total = None
        for k, w in enumerate((w0, w1, w2, w3)):
            term = lax.dot_general(
                d_ref[from_ref[k], :rows, :],
                w[h * feat : (h + 1) * feat, :],
                CONTRACT,
                preferred_element_type=F32,
            )
            total = term if total is None else total + term
        if h:
            give_ref[:rows, :] = total.astype(BF)
            give_ref[rows:, :] = extra_ref[...]
        else:
            keep_ref[...] = total


def give_keep(origin, deltas, weights, extra, rows, feat):
    vmem = pl.BlockSpec(memory_space=pltpu.VMEM)
    return pl.pallas_call(
        give_kernel,
        out_shape=(
            jax.ShapeDtypeStruct((rows + extra.shape[0], feat), BF),
            jax.ShapeDtypeStruct((rows, feat), F32),
        ),
        in_specs=[pl.BlockSpec(memory_space=pltpu.SMEM)] + [vmem] * 6,
        compiler_params=pltpu.CompilerParams(vmem_limit_bytes=VMEM),
        name="input_grads",
    )(origin, deltas, *weights, extra)


def spread_kernel(keep_ref, came_ref, place_ref, gate_ref, out_ref):
    rows, feat = keep_ref.shape
    term = (keep_ref[...] + came_ref[:rows, :].astype(F32)).astype(BF)
    out_ref[:, :feat] = jnp.dot(place_ref[...], term, preferred_element_type=F32).astype(BF)
    block = gate_ref[...]
    slots = out_ref.shape[0]
    block = jnp.broadcast_to(block[None], (slots // SLOTS, SLOTS, 128)).reshape(slots, 128)
    out_ref[:, feat:] = block.astype(BF)


def spread_out(keep, came, place_t, gate_block):
    slots, feat = place_t.shape[0], keep.shape[1]
    return pl.pallas_call(
        spread_kernel,
        out_shape=jax.ShapeDtypeStruct((slots, feat + 128), BF),
        compiler_params=pltpu.CompilerParams(vmem_limit_bytes=VMEM),
        name="rows_to_slots",
    )(keep, came, place_t, gate_block)


def on_device(tokens, output_grad, gate_weight, up_weight, down_weight, chosen, gate_values):
    expert = lax.axis_index("y")
    exp_index = expert * NZ + lax.axis_index("z")
    x_index = lax.axis_index("x")
    c_index = lax.axis_index("c")
    expert_count, capacity = chosen.shape
    token_rows, feat = tokens.shape
    hid = gate_weight.shape[2]
    peers = NY * NZ
    all_slots = peers * SLOTS
    wide = NC * feat

    own_weights = gate_weight[0], up_weight[0], down_weight[0]

    def starts(k):
        dest = (x_index + k) % NX * wide
        return [dest + c_index * feat, dest + (1 - c_index) * feat]

    outgoing, pick, out_2 = pick_rows(
        jnp.stack(starts(2) + [exp_index * token_rows]), chosen, tokens, output_grad, *own_weights
    )
    got = lax.all_to_all(outgoing, ("y", "z"), split_axis=0, concat_axis=0, tiled=True)
    weights = {2: shift_x(out_2, 2)}
    out_1, out_3, weights[0] = pack_weights(
        jnp.stack(starts(1) + starts(3) + starts(0)), *own_weights, feat, BIG_VMEM
    )
    weights[1] = shift_x(out_1, 1)
    weights[3] = shift_x(out_3, 3)
    got, weights[2] = lax.optimization_barrier((got, weights[2]))

    source = chosen // token_rows
    order = jnp.arange(capacity, dtype=jnp.int32)
    my_source = lax.dynamic_index_in_dim(source, expert, 0, keepdims=False)
    my_gates = lax.dynamic_index_in_dim(gate_values, expert, 0, keepdims=False)
    same = (my_source[:, None] == my_source[None, :]) & (order[None, :] < order[:, None])
    my_rank = jnp.sum(same.astype(jnp.int32), axis=1)
    my_slot = my_source * SLOTS + my_rank
    slot_order = jnp.arange(all_slots, dtype=jnp.int32)
    place = (my_slot[:, None] == slot_order[None, :]).astype(BF)
    place_t = (my_slot[None, :] == slot_order[:, None]).astype(BF)
    own = jnp.dot(place, got, preferred_element_type=F32).astype(BF)
    other = swap_cores(own)
    other, weights[1], weights[3] = lax.optimization_barrier((other, weights[1], weights[3]))
    sums = None
    for k in (2, 1, 3, 0):
        part = pre_part(own, other, weights[(NX - k) % NX])
        part = (shift_x(part, k) if k else part).astype(F32)
        sums = part if sums is None else sums + part
    pre_gate, pre_up, back = sums[:, :hid], sums[:, hid : 2 * hid], sums[:, 2 * hid :]
    active, slope = silu_parts(pre_gate)
    gate_part = jnp.sum(active * pre_up * back, axis=1)
    scaled = my_gates[:, None] * back
    gate_delta = (scaled * pre_up * slope).astype(BF)
    up_delta = (scaled * active).astype(BF)
    hi, lo = hi_lo(gate_part)
    extra = jnp.concatenate([hi, lo, jnp.zeros((16 * 2 * hid - 2 * capacity,), BF)]).reshape(16, 2 * hid)
    delta = jnp.concatenate([jnp.concatenate([gate_delta, up_delta], axis=1), extra], axis=0)
    deltas = lax.all_gather(delta, "x", axis=0, tiled=False)
    gate_rows = deltas[:, capacity:].reshape(NX, -1).astype(F32)
    gate_sum = jnp.sum(gate_rows[:, :capacity] + gate_rows[:, capacity : 2 * capacity], axis=0)
    origin = (x_index - jnp.arange(NX, dtype=jnp.int32)) % NX
    hi, lo = hi_lo(gate_sum)
    extra = jnp.concatenate([hi, lo, jnp.zeros((16 * feat - 2 * capacity,), BF)]).reshape(16, feat)
    give, keep = give_keep(
        origin, deltas, [weights[k] for k in range(NX)], extra, capacity, feat
    )
    came = swap_cores(give)
    came_gate = came[capacity:].reshape(-1).astype(F32)
    gate_sum = (hi.astype(F32) + lo.astype(F32)) + (came_gate[:capacity] + came_gate[capacity : 2 * capacity])
    hi, lo = hi_lo(gate_sum)
    gate_block = jnp.concatenate([hi, lo, jnp.zeros((SLOTS * 128 - 2 * capacity,), BF)])
    gate_block = gate_block.astype(F32).reshape(SLOTS, 128)
    home = lax.all_to_all(
        spread_out(keep, came, place_t, gate_block), ("y", "z"), split_axis=0, concat_axis=0, tiled=True
    )
    owner = jnp.broadcast_to(
        pick.reshape(expert_count, 1, SLOTS, token_rows), (expert_count, NZ, SLOTS, token_rows)
    ).reshape(all_slots, token_rows)
    grad_tokens = lax.dot_general(
        owner, home[:, :feat], (((0,), (0,)), ((), ())), preferred_element_type=F32
    ).astype(BF)
    gates = jnp.sum(home[:, feat:].reshape(expert_count, NZ, SLOTS * 128).astype(F32), axis=1)
    gate_grad = gates[:, :capacity] + gates[:, capacity : 2 * capacity]
    return grad_tokens, gate_grad


def solution(mesh):
    grid = Mesh(np.asarray(mesh.devices).reshape(NY, NZ, NX, NC), ("y", "z", "x", "c"))
    exp, ten = ("y", "z"), ("x", "c")
    in_specs = (
        P(exp, ten),
        P(exp, ten),
        P(exp, None, ten),
        P(exp, None, ten),
        P(exp, ten, None),
        P(),
        P(),
    )
    out_specs = (P(exp, ten), P())
    return jax.shard_map(on_device, mesh=grid, in_specs=in_specs, out_specs=out_specs, check_vma=False)
```

```python
import jax
import jax.numpy as jnp
import numpy as np
from jax import lax
from jax.experimental import pallas as pl
from jax.experimental.pallas import tpu as pltpu
from jax.sharding import Mesh
from jax.sharding import PartitionSpec as P

NY, NZ, NX, NC = 8, 8, 4, 2
SLOTS = 8
BF = jnp.bfloat16
F32 = jnp.float32
VMEM = 12 * 1024 * 1024
BIG_VMEM = 60 * 1024 * 1024
CONTRACT = (((1,), (1,)), ((), ()))


def silu_parts(values):
    sig = jax.nn.sigmoid(values)
    return (values * sig, sig * (1.0 + values * (1.0 - sig)))


def swap_cores(a):
    return lax.ppermute(a, "c", [(0, 1), (1, 0)])


def shift_x(a, k):
    return lax.ppermute(a, "x", [(j, (j + k) % NX) for j in range(NX)])


def hi_lo(values):
    hi = values.astype(BF)
    lo = (values - hi.astype(F32)).astype(BF)
    return hi, lo


def start_packing(start_of, gate_ref, up_ref, down_ref, outs, sems):
    hid = gate_ref.shape[1]
    chunk = 2 * hid
    feat = outs[0].shape[0] // 3
    started = []
    for k, out in enumerate(outs):
        for h in range(NC):
            start = pl.multiple_of(start_of(k, h, feat), feat)
            rows = pl.ds(h * feat, feat)
            copies = [
                (gate_ref.at[pl.ds(start, feat), :], out.at[rows, pl.ds(0, hid)]),
                (up_ref.at[pl.ds(start, feat), :], out.at[rows, pl.ds(hid, hid)]),
            ]
            for q in range(feat // chunk):
                begin = pl.multiple_of(start + q * chunk, chunk)
                low = NC * feat + (h * (feat // chunk) + q) * hid
                copies.append((down_ref.at[:, pl.ds(begin, chunk)], out.at[pl.ds(low, hid), :]))
            for src, dst in copies:
                copy = pltpu.make_async_copy(src, dst, sems.at[len(started)])
                copy.start()
                started.append(copy)
    return started


def packed_shape(hid, feat):
    return jax.ShapeDtypeStruct((NC * feat + feat // 2 // hid * NC * hid, 2 * hid), BF)


def pack_copies(hid, feat, count):
    return pltpu.SemaphoreType.DMA((count * NC * (2 + feat // 2 // hid),))


def pack_kernel(where_ref, gate_ref, up_ref, down_ref, *refs):
    for copy in start_packing(lambda k, h, feat: where_ref[k * NC + h], gate_ref, up_ref, down_ref, refs[:-1], refs[-1]):
        copy.wait()


def pack_weights(where, gate, up, down, feat, limit):
    hid = gate.shape[1]
    count = where.shape[0] // NC
    hbm = pl.BlockSpec(memory_space=pltpu.HBM)
    return pl.pallas_call(
        pack_kernel,
        out_shape=(packed_shape(hid, feat),) * count,
        in_specs=[pl.BlockSpec(memory_space=pltpu.SMEM), hbm, hbm, hbm],
        scratch_shapes=[pack_copies(hid, feat, count)],
        compiler_params=pltpu.CompilerParams(vmem_limit_bytes=limit),
        name="pack_weights",
    )(where, gate, up, down)


def pick_kernel(
    chosen_ref, tokens_ref, grads_ref, gate_ref, up_ref, down_ref, rows_ref, pick_ref, out_ref, sems
):
    c_index = lax.axis_index("c")
    dest = lax.rem(lax.axis_index("x") + 2, NX)
    started = start_packing(lambda k, h, feat: (dest * NC + (1 - c_index if h else c_index)) * feat, gate_ref, up_ref, down_ref, [out_ref], sems)
    token_rows, feat = tokens_ref.shape
    experts, capacity = chosen_ref.shape
    local = chosen_ref[...] - (lax.axis_index("y") * NZ + lax.axis_index("z")) * token_rows
    mine = (local >= 0) & (local < token_rows)
    earlier = lax.broadcasted_iota(jnp.int32, (capacity, capacity), 0) < lax.broadcasted_iota(
        jnp.int32, (capacity, capacity), 1
    )
    earlier = jnp.where(earlier, 1.0, 0.0).astype(BF)
    rank = jnp.dot(jnp.where(mine, 1.0, 0.0).astype(BF), earlier, preferred_element_type=F32)
    key = jnp.where(mine, (local + 1).astype(F32), 0.0)
    slot = lax.broadcasted_iota(jnp.int32, (SLOTS, capacity), 0).astype(F32)
    token = lax.broadcasted_iota(jnp.int32, (SLOTS, token_rows), 1).astype(F32) + 1.0
    picks = []
    for e in range(experts):
        hit = slot == jnp.broadcast_to(rank[e : e + 1, :], slot.shape)
        row = jnp.sum(jnp.where(hit, jnp.broadcast_to(key[e : e + 1, :], slot.shape), 0.0), axis=1, keepdims=True)
        picks.append(jnp.where(row == token, 1.0, 0.0))
    pick = jnp.concatenate(picks, axis=0).astype(BF)
    pick_ref[...] = pick
    for i, ref in enumerate((tokens_ref, grads_ref)):
        picked = jnp.dot(pick, ref[...], preferred_element_type=F32)
        picked = picked.reshape(experts, 1, SLOTS, feat)
        picked = jnp.broadcast_to(picked, (experts, NZ, SLOTS, feat)).reshape(experts * NZ * SLOTS, feat)
        rows_ref[:, i * feat : (i + 1) * feat] = picked.astype(BF)
    for copy in started:
        copy.wait()


def pick_rows(chosen, tokens, grads, gate, up, down):
    hid = gate.shape[1]
    hbm = pl.BlockSpec(memory_space=pltpu.HBM)
    token_rows, feat = tokens.shape
    picks = chosen.shape[0] * SLOTS
    vmem = pl.BlockSpec(memory_space=pltpu.VMEM)
    return pl.pallas_call(
        pick_kernel,
        out_shape=(
            jax.ShapeDtypeStruct((picks * NZ, 2 * feat), BF),
            jax.ShapeDtypeStruct((picks, token_rows), BF),
            packed_shape(hid, feat),
        ),
        in_specs=[vmem, vmem, vmem, hbm, hbm, hbm],
        scratch_shapes=[pack_copies(hid, feat, 1)],
        compiler_params=pltpu.CompilerParams(vmem_limit_bytes=BIG_VMEM),
        name="pick_rows",
    )(chosen, tokens, grads, gate, up, down)


def pre_kernel(own_ref, other_ref, w_ref, out_ref):
    feat = own_ref.shape[1] // 2
    chunk = w_ref.shape[1]
    hid = chunk // 2
    gu = None
    back = None
    for h, rows in enumerate((own_ref, other_ref)):
        term = jnp.dot(rows[:, :feat], w_ref[h * feat : (h + 1) * feat, :], preferred_element_type=F32)
        gu = term if gu is None else gu + term
        for q in range(feat // chunk):
            low = NC * feat + (h * (feat // chunk) + q) * hid
            term = lax.dot_general(
                rows[:, feat + q * chunk : feat + (q + 1) * chunk],
                w_ref[low : low + hid, :],
                CONTRACT,
                preferred_element_type=F32,
            )
            back = term if back is None else back + term
    out_ref[:, :chunk] = gu.astype(BF)
    out_ref[:, chunk:] = back.astype(BF)


def pre_part(own, other, w):
    rows = own.shape[0]
    return pl.pallas_call(
        pre_kernel,
        out_shape=jax.ShapeDtypeStruct((rows, w.shape[1] // 2 * 3), BF),
        compiler_params=pltpu.CompilerParams(vmem_limit_bytes=VMEM),
        name="pre_part",
    )(own, other, w)


def half_term(h, from_ref, d_ref, weights, rows, feat):
    total = None
    for k, w in enumerate(weights):
        term = lax.dot_general(
            d_ref[from_ref[k], :rows, :],
            w[h * feat : (h + 1) * feat, :],
            CONTRACT,
            preferred_element_type=F32,
        )
        total = term if total is None else total + term
    return total


def give_kernel(from_ref, d_ref, w0, w1, w2, w3, extra_ref, give_ref):
    rows = give_ref.shape[0] - extra_ref.shape[0]
    total = half_term(1, from_ref, d_ref, (w0, w1, w2, w3), rows, give_ref.shape[1])
    give_ref[:rows, :] = total.astype(BF)
    give_ref[rows:, :] = extra_ref[...]


def keep_kernel(from_ref, d_ref, w0, w1, w2, w3, keep_ref):
    rows, feat = keep_ref.shape
    keep_ref[...] = half_term(0, from_ref, d_ref, (w0, w1, w2, w3), rows, feat)


def give_keep(origin, deltas, weights, extra, rows, feat):
    vmem = pl.BlockSpec(memory_space=pltpu.VMEM)
    smem = pl.BlockSpec(memory_space=pltpu.SMEM)
    give = pl.pallas_call(
        give_kernel,
        out_shape=jax.ShapeDtypeStruct((rows + extra.shape[0], feat), BF),
        in_specs=[smem] + [vmem] * 6,
        compiler_params=pltpu.CompilerParams(vmem_limit_bytes=VMEM),
        name="input_grads_give",
    )(origin, deltas, *weights, extra)
    keep = pl.pallas_call(
        keep_kernel,
        out_shape=jax.ShapeDtypeStruct((rows, feat), F32),
        in_specs=[smem] + [vmem] * 5,
        compiler_params=pltpu.CompilerParams(vmem_limit_bytes=VMEM),
        name="input_grads_keep",
    )(origin, deltas, *weights)
    return give, keep


def spread_kernel(keep_ref, came_ref, place_ref, gate_ref, out_ref):
    rows, feat = keep_ref.shape
    term = (keep_ref[...] + came_ref[:rows, :].astype(F32)).astype(BF)
    out_ref[:, :feat] = jnp.dot(place_ref[...], term, preferred_element_type=F32).astype(BF)
    block = gate_ref[...]
    slots = out_ref.shape[0]
    block = jnp.broadcast_to(block[None], (slots // SLOTS, SLOTS, 128)).reshape(slots, 128)
    out_ref[:, feat:] = block.astype(BF)


def spread_out(keep, came, place_t, gate_block):
    slots, feat = place_t.shape[0], keep.shape[1]
    return pl.pallas_call(
        spread_kernel,
        out_shape=jax.ShapeDtypeStruct((slots, feat + 128), BF),
        compiler_params=pltpu.CompilerParams(vmem_limit_bytes=VMEM),
        name="rows_to_slots",
    )(keep, came, place_t, gate_block)


def on_device(tokens, output_grad, gate_weight, up_weight, down_weight, chosen, gate_values):
    expert = lax.axis_index("y")
    exp_index = expert * NZ + lax.axis_index("z")
    x_index = lax.axis_index("x")
    c_index = lax.axis_index("c")
    expert_count, capacity = chosen.shape
    token_rows, feat = tokens.shape
    hid = gate_weight.shape[2]
    peers = NY * NZ
    all_slots = peers * SLOTS
    wide = NC * feat

    own_weights = gate_weight[0], up_weight[0], down_weight[0]

    def starts(k):
        dest = (x_index + k) % NX * wide
        return [dest + c_index * feat, dest + (1 - c_index) * feat]

    outgoing, pick, out_2 = pick_rows(chosen, tokens, output_grad, *own_weights)
    got = lax.all_to_all(outgoing, ("y", "z"), split_axis=0, concat_axis=0, tiled=True)
    weights = {2: shift_x(out_2, 2)}
    out_1, out_3, weights[0] = pack_weights(
        jnp.stack(starts(1) + starts(3) + starts(0)), *own_weights, feat, BIG_VMEM
    )
    weights[1] = shift_x(out_1, 1)
    weights[3] = shift_x(out_3, 3)
    got, weights[2] = lax.optimization_barrier((got, weights[2]))

    source = chosen // token_rows
    order = jnp.arange(capacity, dtype=jnp.int32)
    my_source = lax.dynamic_index_in_dim(source, expert, 0, keepdims=False)
    my_gates = lax.dynamic_index_in_dim(gate_values, expert, 0, keepdims=False)
    same = (my_source[:, None] == my_source[None, :]) & (order[None, :] < order[:, None])
    my_rank = jnp.sum(same.astype(jnp.int32), axis=1)
    my_slot = my_source * SLOTS + my_rank
    slot_order = jnp.arange(all_slots, dtype=jnp.int32)
    place = (my_slot[:, None] == slot_order[None, :]).astype(BF)
    place_t = (my_slot[None, :] == slot_order[:, None]).astype(BF)
    own = jnp.dot(place, got, preferred_element_type=F32).astype(BF)
    other = swap_cores(own)
    other, weights[1], weights[3] = lax.optimization_barrier((other, weights[1], weights[3]))
    sums = None
    for k in (2, 1, 3, 0):
        part = pre_part(own, other, weights[(NX - k) % NX])
        part = (shift_x(part, k) if k else part).astype(F32)
        sums = part if sums is None else sums + part
    pre_gate, pre_up, back = sums[:, :hid], sums[:, hid : 2 * hid], sums[:, 2 * hid :]
    active, slope = silu_parts(pre_gate)
    gate_part = jnp.sum(active * pre_up * back, axis=1)
    scaled = my_gates[:, None] * back
    gate_delta = (scaled * pre_up * slope).astype(BF)
    up_delta = (scaled * active).astype(BF)
    hi, lo = hi_lo(gate_part)
    extra = jnp.concatenate([hi, lo, jnp.zeros((16 * 2 * hid - 2 * capacity,), BF)]).reshape(16, 2 * hid)
    delta = jnp.concatenate([jnp.concatenate([gate_delta, up_delta], axis=1), extra], axis=0)
    deltas = lax.all_gather(delta, "x", axis=0, tiled=False)
    gate_rows = deltas[:, capacity:].reshape(NX, -1).astype(F32)
    gate_sum = jnp.sum(gate_rows[:, :capacity] + gate_rows[:, capacity : 2 * capacity], axis=0)
    origin = (x_index - jnp.arange(NX, dtype=jnp.int32)) % NX
    hi, lo = hi_lo(gate_sum)
    extra = jnp.concatenate([hi, lo, jnp.zeros((16 * feat - 2 * capacity,), BF)]).reshape(16, feat)
    give, keep = give_keep(
        origin, deltas, [weights[k] for k in range(NX)], extra, capacity, feat
    )
    came = swap_cores(give)
    came_gate = came[capacity:].reshape(-1).astype(F32)
    gate_sum = (hi.astype(F32) + lo.astype(F32)) + (came_gate[:capacity] + came_gate[capacity : 2 * capacity])
    hi, lo = hi_lo(gate_sum)
    gate_block = jnp.concatenate([hi, lo, jnp.zeros((SLOTS * 128 - 2 * capacity,), BF)])
    gate_block = gate_block.astype(F32).reshape(SLOTS, 128)
    home = lax.all_to_all(
        spread_out(keep, came, place_t, gate_block), ("y", "z"), split_axis=0, concat_axis=0, tiled=True
    )
    owner = jnp.broadcast_to(
        pick.reshape(expert_count, 1, SLOTS, token_rows), (expert_count, NZ, SLOTS, token_rows)
    ).reshape(all_slots, token_rows)
    grad_tokens = lax.dot_general(
        owner, home[:, :feat], (((0,), (0,)), ((), ())), preferred_element_type=F32
    ).astype(BF)
    gates = jnp.sum(home[:, feat:].reshape(expert_count, NZ, SLOTS * 128).astype(F32), axis=1)
    gate_grad = gates[:, :capacity] + gates[:, capacity : 2 * capacity]
    return grad_tokens, gate_grad


def solution(mesh):
    grid = Mesh(np.asarray(mesh.devices).reshape(NY, NZ, NX, NC), ("y", "z", "x", "c"))
    exp, ten = ("y", "z"), ("x", "c")
    in_specs = (
        P(exp, ten),
        P(exp, ten),
        P(exp, None, ten),
        P(exp, None, ten),
        P(exp, ten, None),
        P(),
        P(),
    )
    out_specs = (P(exp, ten), P())
    return jax.shard_map(on_device, mesh=grid, in_specs=in_specs, out_specs=out_specs, check_vma=False)
```

```python
import jax
import jax.numpy as jnp
import numpy as np
from jax import lax
from jax.experimental import pallas as pl
from jax.experimental.pallas import tpu as pltpu
from jax.sharding import Mesh
from jax.sharding import PartitionSpec as P

NY, NZ, NX, NC = 8, 8, 4, 2
SLOTS = 8
BF = jnp.bfloat16
F32 = jnp.float32
VMEM = 6 * 1024 * 1024
BIG_VMEM = 60 * 1024 * 1024
CONTRACT = (((1,), (1,)), ((), ()))


def silu_parts(values):
    sig = jax.nn.sigmoid(values)
    return (values * sig, sig * (1.0 + values * (1.0 - sig)))


def swap_cores(a):
    return lax.ppermute(a, "c", [(0, 1), (1, 0)])


def shift_x(a, k):
    return lax.ppermute(a, "x", [(j, (j + k) % NX) for j in range(NX)])


def hi_lo(values):
    hi = values.astype(BF)
    lo = (values - hi.astype(F32)).astype(BF)
    return hi, lo


def start_packing(start_of, gate_ref, up_ref, down_ref, outs, sems):
    hid = gate_ref.shape[1]
    chunk = 2 * hid
    feat = outs[0].shape[0] // 3
    started = []
    for k, out in enumerate(outs):
        for h in range(NC):
            start = pl.multiple_of(start_of(k, h, feat), feat)
            rows = pl.ds(h * feat, feat)
            copies = [
                (gate_ref.at[pl.ds(start, feat), :], out.at[rows, pl.ds(0, hid)]),
                (up_ref.at[pl.ds(start, feat), :], out.at[rows, pl.ds(hid, hid)]),
            ]
            for q in range(feat // chunk):
                begin = pl.multiple_of(start + q * chunk, chunk)
                low = NC * feat + (h * (feat // chunk) + q) * hid
                copies.append((down_ref.at[:, pl.ds(begin, chunk)], out.at[pl.ds(low, hid), :]))
            for src, dst in copies:
                copy = pltpu.make_async_copy(src, dst, sems.at[len(started)])
                copy.start()
                started.append(copy)
    return started


def packed_shape(hid, feat):
    return jax.ShapeDtypeStruct((NC * feat + feat // 2 // hid * NC * hid, 2 * hid), BF)


def pack_copies(hid, feat, count):
    return pltpu.SemaphoreType.DMA((count * NC * (2 + feat // 2 // hid),))


def pack_kernel(where_ref, gate_ref, up_ref, down_ref, *refs):
    for copy in start_packing(lambda k, h, feat: where_ref[k * NC + h], gate_ref, up_ref, down_ref, refs[:-1], refs[-1]):
        copy.wait()


def pack_weights(where, gate, up, down, feat, limit):
    hid = gate.shape[1]
    count = where.shape[0] // NC
    hbm = pl.BlockSpec(memory_space=pltpu.HBM)
    return pl.pallas_call(
        pack_kernel,
        out_shape=(packed_shape(hid, feat),) * count,
        in_specs=[pl.BlockSpec(memory_space=pltpu.SMEM), hbm, hbm, hbm],
        scratch_shapes=[pack_copies(hid, feat, count)],
        compiler_params=pltpu.CompilerParams(vmem_limit_bytes=limit),
        name="pack_weights",
    )(where, gate, up, down)


def pick_kernel(
    chosen_ref, tokens_ref, grads_ref, gate_ref, up_ref, down_ref, rows_ref, pick_ref, out_ref, sems
):
    c_index = lax.axis_index("c")
    dest = lax.rem(lax.axis_index("x") + 2, NX)
    started = start_packing(lambda k, h, feat: (dest * NC + (1 - c_index if h else c_index)) * feat, gate_ref, up_ref, down_ref, [out_ref], sems)
    token_rows, feat = tokens_ref.shape
    experts, capacity = chosen_ref.shape
    local = chosen_ref[...] - (lax.axis_index("y") * NZ + lax.axis_index("z")) * token_rows
    mine = (local >= 0) & (local < token_rows)
    earlier = lax.broadcasted_iota(jnp.int32, (capacity, capacity), 0) < lax.broadcasted_iota(
        jnp.int32, (capacity, capacity), 1
    )
    earlier = jnp.where(earlier, 1.0, 0.0).astype(BF)
    rank = jnp.dot(jnp.where(mine, 1.0, 0.0).astype(BF), earlier, preferred_element_type=F32)
    key = jnp.where(mine, (local + 1).astype(F32), 0.0)
    slot = lax.broadcasted_iota(jnp.int32, (SLOTS, capacity), 0).astype(F32)
    token = lax.broadcasted_iota(jnp.int32, (SLOTS, token_rows), 1).astype(F32) + 1.0
    picks = []
    for e in range(experts):
        hit = slot == jnp.broadcast_to(rank[e : e + 1, :], slot.shape)
        row = jnp.sum(jnp.where(hit, jnp.broadcast_to(key[e : e + 1, :], slot.shape), 0.0), axis=1, keepdims=True)
        picks.append(jnp.where(row == token, 1.0, 0.0))
    pick = jnp.concatenate(picks, axis=0).astype(BF)
    pick_ref[...] = pick
    for i, ref in enumerate((tokens_ref, grads_ref)):
        picked = jnp.dot(pick, ref[...], preferred_element_type=F32)
        picked = picked.reshape(experts, 1, SLOTS, feat)
        picked = jnp.broadcast_to(picked, (experts, NZ, SLOTS, feat)).reshape(experts * NZ * SLOTS, feat)
        rows_ref[:, i * feat : (i + 1) * feat] = picked.astype(BF)
    for copy in started:
        copy.wait()


def pick_rows(chosen, tokens, grads, gate, up, down):
    hid = gate.shape[1]
    hbm = pl.BlockSpec(memory_space=pltpu.HBM)
    token_rows, feat = tokens.shape
    picks = chosen.shape[0] * SLOTS
    vmem = pl.BlockSpec(memory_space=pltpu.VMEM)
    return pl.pallas_call(
        pick_kernel,
        out_shape=(
            jax.ShapeDtypeStruct((picks * NZ, 2 * feat), BF),
            jax.ShapeDtypeStruct((picks, token_rows), BF),
            packed_shape(hid, feat),
        ),
        in_specs=[vmem, vmem, vmem, hbm, hbm, hbm],
        scratch_shapes=[pack_copies(hid, feat, 1)],
        compiler_params=pltpu.CompilerParams(vmem_limit_bytes=BIG_VMEM),
        name="pick_rows",
    )(chosen, tokens, grads, gate, up, down)


def pre_kernel(own_ref, other_ref, w_ref, out_ref):
    feat = own_ref.shape[1] // 2
    chunk = w_ref.shape[1]
    hid = chunk // 2
    gu = None
    back = None
    for h, rows in enumerate((own_ref, other_ref)):
        term = jnp.dot(rows[:, :feat], w_ref[h * feat : (h + 1) * feat, :], preferred_element_type=F32)
        gu = term if gu is None else gu + term
        for q in range(feat // chunk):
            low = NC * feat + (h * (feat // chunk) + q) * hid
            term = lax.dot_general(
                rows[:, feat + q * chunk : feat + (q + 1) * chunk],
                w_ref[low : low + hid, :],
                CONTRACT,
                preferred_element_type=F32,
            )
            back = term if back is None else back + term
    out_ref[:, :chunk] = gu.astype(BF)
    out_ref[:, chunk:] = back.astype(BF)


def pre_part(own, other, w):
    rows = own.shape[0]
    return pl.pallas_call(
        pre_kernel,
        out_shape=jax.ShapeDtypeStruct((rows, w.shape[1] // 2 * 3), BF),
        compiler_params=pltpu.CompilerParams(vmem_limit_bytes=VMEM),
        name="pre_part",
    )(own, other, w)


def half_term(h, from_ref, d_ref, weights, rows, feat):
    total = None
    for k, w in enumerate(weights):
        term = lax.dot_general(
            d_ref[from_ref[k], :rows, :],
            w[h * feat : (h + 1) * feat, :],
            CONTRACT,
            preferred_element_type=F32,
        )
        total = term if total is None else total + term
    return total


def give_kernel(from_ref, d_ref, w0, w1, w2, w3, extra_ref, give_ref):
    rows = give_ref.shape[0] - extra_ref.shape[0]
    total = half_term(1, from_ref, d_ref, (w0, w1, w2, w3), rows, give_ref.shape[1])
    give_ref[:rows, :] = total.astype(BF)
    give_ref[rows:, :] = extra_ref[...]


def keep_kernel(from_ref, d_ref, w0, w1, w2, w3, keep_ref):
    rows, feat = keep_ref.shape
    keep_ref[...] = half_term(0, from_ref, d_ref, (w0, w1, w2, w3), rows, feat)


def give_keep(origin, deltas, weights, extra, rows, feat):
    vmem = pl.BlockSpec(memory_space=pltpu.VMEM)
    smem = pl.BlockSpec(memory_space=pltpu.SMEM)
    give = pl.pallas_call(
        give_kernel,
        out_shape=jax.ShapeDtypeStruct((rows + extra.shape[0], feat), BF),
        in_specs=[smem] + [vmem] * 6,
        compiler_params=pltpu.CompilerParams(vmem_limit_bytes=VMEM),
        name="input_grads_give",
    )(origin, deltas, *weights, extra)
    keep = pl.pallas_call(
        keep_kernel,
        out_shape=jax.ShapeDtypeStruct((rows, feat), F32),
        in_specs=[smem] + [vmem] * 5,
        compiler_params=pltpu.CompilerParams(vmem_limit_bytes=VMEM),
        name="input_grads_keep",
    )(origin, deltas, *weights)
    return give, keep


def spread_kernel(keep_ref, came_ref, place_ref, gate_ref, out_ref):
    rows, feat = keep_ref.shape
    term = (keep_ref[...] + came_ref[:rows, :].astype(F32)).astype(BF)
    out_ref[:, :feat] = jnp.dot(place_ref[...], term, preferred_element_type=F32).astype(BF)
    block = gate_ref[...]
    slots = out_ref.shape[0]
    block = jnp.broadcast_to(block[None], (slots // SLOTS, SLOTS, 128)).reshape(slots, 128)
    out_ref[:, feat:] = block.astype(BF)


def spread_out(keep, came, place_t, gate_block):
    slots, feat = place_t.shape[0], keep.shape[1]
    return pl.pallas_call(
        spread_kernel,
        out_shape=jax.ShapeDtypeStruct((slots, feat + 128), BF),
        compiler_params=pltpu.CompilerParams(vmem_limit_bytes=VMEM),
        name="rows_to_slots",
    )(keep, came, place_t, gate_block)


def on_device(tokens, output_grad, gate_weight, up_weight, down_weight, chosen, gate_values):
    expert = lax.axis_index("y")
    exp_index = expert * NZ + lax.axis_index("z")
    x_index = lax.axis_index("x")
    c_index = lax.axis_index("c")
    expert_count, capacity = chosen.shape
    token_rows, feat = tokens.shape
    hid = gate_weight.shape[2]
    peers = NY * NZ
    all_slots = peers * SLOTS
    wide = NC * feat

    own_weights = gate_weight[0], up_weight[0], down_weight[0]

    def starts(k):
        dest = (x_index + k) % NX * wide
        return [dest + c_index * feat, dest + (1 - c_index) * feat]

    outgoing, pick, out_2 = pick_rows(chosen, tokens, output_grad, *own_weights)
    got = lax.all_to_all(outgoing, ("y", "z"), split_axis=0, concat_axis=0, tiled=True)
    weights = {2: shift_x(out_2, 2)}
    out_1, out_3, weights[0] = pack_weights(
        jnp.stack(starts(1) + starts(3) + starts(0)), *own_weights, feat, BIG_VMEM
    )
    weights[1] = shift_x(out_1, 1)
    weights[3] = shift_x(out_3, 3)
    got, weights[2] = lax.optimization_barrier((got, weights[2]))

    source = chosen // token_rows
    order = jnp.arange(capacity, dtype=jnp.int32)
    my_source = lax.dynamic_index_in_dim(source, expert, 0, keepdims=False)
    my_gates = lax.dynamic_index_in_dim(gate_values, expert, 0, keepdims=False)
    same = (my_source[:, None] == my_source[None, :]) & (order[None, :] < order[:, None])
    my_rank = jnp.sum(same.astype(jnp.int32), axis=1)
    my_slot = my_source * SLOTS + my_rank
    slot_order = jnp.arange(all_slots, dtype=jnp.int32)
    place = (my_slot[:, None] == slot_order[None, :]).astype(BF)
    place_t = (my_slot[None, :] == slot_order[:, None]).astype(BF)
    own = jnp.dot(place, got, preferred_element_type=F32).astype(BF)
    other = swap_cores(own)
    other, weights[1], weights[3] = lax.optimization_barrier((other, weights[1], weights[3]))
    sums = None
    for k in (2, 1, 3, 0):
        part = pre_part(own, other, weights[(NX - k) % NX])
        part = (shift_x(part, k) if k else part).astype(F32)
        sums = part if sums is None else sums + part
    pre_gate, pre_up, back = sums[:, :hid], sums[:, hid : 2 * hid], sums[:, 2 * hid :]
    active, slope = silu_parts(pre_gate)
    gate_part = jnp.sum(active * pre_up * back, axis=1)
    scaled = my_gates[:, None] * back
    gate_delta = (scaled * pre_up * slope).astype(BF)
    up_delta = (scaled * active).astype(BF)
    hi, lo = hi_lo(gate_part)
    extra = jnp.concatenate([hi, lo, jnp.zeros((16 * 2 * hid - 2 * capacity,), BF)]).reshape(16, 2 * hid)
    delta = jnp.concatenate([jnp.concatenate([gate_delta, up_delta], axis=1), extra], axis=0)
    deltas = lax.all_gather(delta, "x", axis=0, tiled=False)
    gate_rows = deltas[:, capacity:].reshape(NX, -1).astype(F32)
    gate_sum = jnp.sum(gate_rows[:, :capacity] + gate_rows[:, capacity : 2 * capacity], axis=0)
    origin = (x_index - jnp.arange(NX, dtype=jnp.int32)) % NX
    hi, lo = hi_lo(gate_sum)
    extra = jnp.concatenate([hi, lo, jnp.zeros((16 * feat - 2 * capacity,), BF)]).reshape(16, feat)
    give, keep = give_keep(
        origin, deltas, [weights[k] for k in range(NX)], extra, capacity, feat
    )
    came = swap_cores(give)
    came_gate = came[capacity:].reshape(-1).astype(F32)
    gate_sum = (hi.astype(F32) + lo.astype(F32)) + (came_gate[:capacity] + came_gate[capacity : 2 * capacity])
    hi, lo = hi_lo(gate_sum)
    gate_block = jnp.concatenate([hi, lo, jnp.zeros((SLOTS * 128 - 2 * capacity,), BF)])
    gate_block = gate_block.astype(F32).reshape(SLOTS, 128)
    home = lax.all_to_all(
        spread_out(keep, came, place_t, gate_block), ("y", "z"), split_axis=0, concat_axis=0, tiled=True
    )
    owner = jnp.broadcast_to(
        pick.reshape(expert_count, 1, SLOTS, token_rows), (expert_count, NZ, SLOTS, token_rows)
    ).reshape(all_slots, token_rows)
    grad_tokens = lax.dot_general(
        owner, home[:, :feat], (((0,), (0,)), ((), ())), preferred_element_type=F32
    ).astype(BF)
    gates = jnp.sum(home[:, feat:].reshape(expert_count, NZ, SLOTS * 128).astype(F32), axis=1)
    gate_grad = gates[:, :capacity] + gates[:, capacity : 2 * capacity]
    return grad_tokens, gate_grad


def solution(mesh):
    grid = Mesh(np.asarray(mesh.devices).reshape(NY, NZ, NX, NC), ("y", "z", "x", "c"))
    exp, ten = ("y", "z"), ("x", "c")
    in_specs = (
        P(exp, ten),
        P(exp, ten),
        P(exp, None, ten),
        P(exp, None, ten),
        P(exp, ten, None),
        P(),
        P(),
    )
    out_specs = (P(exp, ten), P())
    return jax.shard_map(on_device, mesh=grid, in_specs=in_specs, out_specs=out_specs, check_vma=False)
```
